32 devices in a mesh: section: 2 (over core), replica: 4 (over z), shard: 4 (over y, x).
Axes of the slice: x: 2, y: 2, z: 4, core: 2. Of those that a mesh axis runs over, the one named last changes fastest.
Arguments:
- inputs: bfloat16 [2, 4, 1024, 1088], P(None, 'replica', 'shard'), may hold values from -6 to 6
- cotangent: bfloat16 [2, 4, 1024, 1088], P(None, 'replica', 'shard'), may hold values from -6 to 6
- segments: int32 [2, 4, 1024], P(None, 'replica'), may hold values from 0 to 3, as said below
- ln1_gain: bfloat16 [2, 1088], P('section', 'shard'), may hold values from 0.5 to 1.5
- ln1_bias: bfloat16 [2, 1088], P('section', 'shard'), may hold values from -1.5 to 1.5
- w_qkv: bfloat16 [2, 1088, 3264], P('section', 'shard'), may hold values from -0.1875 to 0.1875
- w_out: bfloat16 [2, 1088, 1088], P('section', 'shard'), may hold values from -0.75 to 0.75
- out_bias: bfloat16 [2, 1088], P('section', 'shard'), may hold values from -1.5 to 1.5
- ln2_gain: bfloat16 [2, 1088], P('section', 'shard'), may hold values from 0.5 to 1.5
- ln2_bias: bfloat16 [2, 1088], P('section', 'shard'), may hold values from -1.5 to 1.5
- w_up: bfloat16 [2, 1088, 4352], P('section', 'shard'), may hold values from -0.1875 to 0.1875
- up_bias: bfloat16 [2, 4352], P('section', 'shard'), may hold values from -1.5 to 1.5
- w_down: bfloat16 [2, 4352, 1088], P('section', 'shard'), may hold values from -0.09375 to 0.09375
- down_bias: bfloat16 [2, 1088], P('section', 'shard'), may hold values from -1.5 to 1.5
Outputs:
- section_outputs: bfloat16 [2, 2, 4, 1024, 1088], P('section', None, 'replica', 'shard')
- input_grads: bfloat16 [2, 2, 4, 1024, 1088], P('section', None, 'replica', 'shard')
- grad_ln1_gain: float32 [2, 1088], P('section', 'shard')
- grad_ln1_bias: float32 [2, 1088], P('section', 'shard')
- grad_w_qkv: float32 [2, 1088, 3264], P('section', 'shard')
- grad_w_out: float32 [2, 1088, 1088], P('section', 'shard')
- grad_out_bias: float32 [2, 1088], P('section', 'shard')
- grad_ln2_gain: float32 [2, 1088], P('section', 'shard')
- grad_ln2_bias: float32 [2, 1088], P('section', 'shard')
- grad_w_up: float32 [2, 1088, 4352], P('section', 'shard')
- grad_up_bias: float32 [2, 4352], P('section', 'shard')
- grad_w_down: float32 [2, 4352, 1088], P('section', 'shard')
- grad_down_bias: float32 [2, 1088], P('section', 'shard')
The draws below stay inside these ranges and needn't reach their ends.
Inputs may be any that keep to these rules, and one draw needn't show every extreme that they name: `segments`: in every sequence the document number starts at 0 at the first token and never falls; of the 2 sequences that share a replica index, one is a single document and every other one holds exactly four documents.
All inputs are finite; a program needn't handle non-finite values.
Results may differ from the reference program's by a relative error of at most 0.015.
Values may be sent and summed in bfloat16 or wider, within the bound.
No kernel may reach another device: no remote copies, remote signals or barrier semaphores. Data moves between devices by JAX's collectives and lax.ppermute only.
A program may use at most 384 MiB of HBM per device.

```python
import math
import jax
import jax.numpy as jnp
from jax import lax

D = 1088
HD = 64
FF = 4352
L = 1024
MB = 2
SEQ_REP = 1
SEQS = 4


def draw_segments(key, part):
    key = jax.random.fold_in(key, 11)
    seq_keys = jax.random.split(jax.random.fold_in(key, 1), MB * SEQS)
    bounds = jax.vmap(lambda one_key: jax.random.permutation(one_key, L - 1)[:3] + 1)(seq_keys)
    bounds = bounds.reshape(MB, SEQS, 3)
    places = jnp.arange(L)
    numbers = jnp.sum((places[None, None, :, None] >= bounds[:, :, None, :]).astype(jnp.int32), axis=3)
    chosen = jax.random.randint(jax.random.fold_in(key, 2), (SEQS // SEQ_REP,), 0, MB * SEQ_REP)
    slot_index = jnp.arange(MB)[:, None] * SEQ_REP + (jnp.arange(SEQS) % SEQ_REP)[None, :]
    group_pick = chosen[jnp.arange(SEQS) // SEQ_REP]
    single = group_pick[None, :] == slot_index
    return jnp.where(single[:, :, None], 0, numbers).astype(jnp.int32)


def level_of(key, extent, shards, least, largest):
    def one(position, blocks):
        draws = jax.random.uniform(jax.random.fold_in(jax.random.fold_in(key, 6), position), (blocks,), jnp.float32, least / len(shards), largest / len(shards))
        return jnp.repeat(jnp.exp(draws), extent[position] // blocks).reshape((-1,) + (1,) * (len(extent) - position - 1))

    level = one(*shards[0])
    for cut in shards[1:]:
        level = level * one(*cut)
    return level


def bell_draw(stream_key, extent, deviation, bound, pieces=(), dtype=jnp.bfloat16):
    loudness = level_of(stream_key, extent, pieces, -0.22, 0.18) if pieces else 1.0
    array = jax.random.normal(stream_key, extent, jnp.float32) * deviation * loudness
    return jnp.minimum(jnp.maximum(array, -bound), bound).astype(dtype)


def setup_inputs(seed: int = 0) -> dict:
    key_list = jax.random.split(jax.random.key(seed), 15)
    return {
        "inputs": bell_draw(key_list[0], (MB, SEQS, L, D), 1.0, 6.0, ((1, 4), (2, 4))),
        "cotangent": bell_draw(key_list[1], (MB, SEQS, L, D), 1.0, 6.0, ((1, 4), (2, 4))),
        "segments": draw_segments(jax.random.fold_in(key_list[14], 71), 0),
        "ln1_gain": jnp.clip(1.0 + 0.1 * jax.random.normal(key_list[3], (2, D), jnp.float32), 0.5, 1.5).astype(jnp.bfloat16),
        "ln1_bias": bell_draw(key_list[4], (2, D), 0.3, 1.5, ((0, 2), (1, 4))),
        "w_qkv": bell_draw(key_list[5], (2, D, 3 * D), D ** -0.5, 0.1875, ((0, 2), (1, 4))),
        "w_out": bell_draw(key_list[6], (2, D, D), (D // 16) ** -0.5, 0.75, ((0, 2), (1, 4))),
        "out_bias": bell_draw(key_list[7], (2, D), 0.3, 1.5, ((0, 2), (1, 4))),
        "ln2_gain": jnp.clip(1.0 + 0.1 * jax.random.normal(key_list[8], (2, D), jnp.float32), 0.5, 1.5).astype(jnp.bfloat16),
        "ln2_bias": bell_draw(key_list[9], (2, D), 0.3, 1.5, ((0, 2), (1, 4))),
        "w_up": bell_draw(key_list[10], (2, D, FF), D ** -0.5, 0.1875, ((0, 2), (1, 4))),
        "up_bias": bell_draw(key_list[11], (2, FF), 0.3, 1.5, ((0, 2), (1, 4))),
        "w_down": bell_draw(key_list[12], (2, FF, D), FF ** -0.5, 0.09375, ((0, 2), (1, 4))),
        "down_bias": bell_draw(key_list[13], (2, D), 0.3, 1.5, ((0, 2), (1, 4))),
    }


norm_eps = 1e-05
highest = lax.Precision.HIGHEST

@jax.custom_vjp
def low(v):
    return lax.optimization_barrier(v.astype(jnp.bfloat16)).astype(jnp.float32)

@jax.custom_vjp
def low_back(v):
    return v

def low_keep(v):
    return (low(v), None)

def low_pass(kept, grad):
    return (grad,)

def back_keep(v):
    return (v, None)

def back_low(kept, grad):
    return (low(grad),)
low.defvjp(low_keep, low_pass)
low_back.defvjp(back_keep, back_low)

def layer_norm(values, gain, bias):
    centre = lax.optimization_barrier(jnp.mean(values, -1, keepdims=True))
    centered = values - centre
    spread = lax.optimization_barrier(jnp.mean(centered * centered, -1, keepdims=True))
    return centered * lax.rsqrt(spread + norm_eps) * gain + bias

def product(left, right):
    return jnp.dot(left, right, precision=highest)

def one_layer(weights, hidden, segment):
    gain_one, bias_one, proj_qkv, proj_out, bias_out, gain_two, bias_two, proj_up, bias_up, proj_down, bias_down = weights
    length, width = hidden.shape
    heads = width // HD
    normed = low(layer_norm(hidden, gain_one, bias_one))
    project = low(low_back(product(normed, proj_qkv)))
    queries = project[:, :width].reshape(length, heads, HD)
    keys = project[:, width:2 * width].reshape(length, heads, HD)
    values = project[:, 2 * width:].reshape(length, heads, HD)
    scores = jnp.einsum('qhd,khd->hqk', queries, keys, precision=highest) * (1.0 / math.sqrt(HD))
    places = jnp.arange(length)
    allowed = (segment[:, None] == segment[None, :]) & (places[None, :] <= places[:, None])
    scores = low_back(jnp.where(allowed[None], scores, -1e+30))
    peak = lax.optimization_barrier(jnp.max(scores, -1, keepdims=True))
    raised = jnp.exp(scores - peak)
    probs = raised / lax.optimization_barrier(jnp.sum(raised, -1, keepdims=True))
    mixed = jnp.einsum('hqk,khd->qhd', low(probs), values, precision=highest).reshape(length, width)
    mixed = low(low_back(mixed))
    middle = hidden + low_back(product(mixed, proj_out) + bias_out)
    normed_two = low(layer_norm(middle, gain_two, bias_two))
    gate_in = low_back(product(normed_two, proj_up) + bias_up)
    activated = low(jax.nn.gelu(gate_in, approximate=True))
    return middle + low_back(product(activated, proj_down) + bias_down)

def reference(inputs, cotangent, segments, ln1_gain, ln1_bias, w_qkv, w_out, out_bias, ln2_gain, ln2_bias, w_up, up_bias, w_down, down_bias):
    params = tuple((item.astype(jnp.float32) for item in (ln1_gain, ln1_bias, w_qkv, w_out, out_bias, ln2_gain, ln2_bias, w_up, up_bias, w_down, down_bias)))
    mb_count, seq_count, length, width = inputs.shape
    flat_in = inputs.astype(jnp.float32).reshape(-1, length, width)
    flat_seg = segments.reshape(-1, length)
    probes = jnp.zeros_like(flat_in)

    def whole(weights, hidden_all, probe_all):

        def per_sequence(item):
            hidden, probe, segment = item
            first_w = tuple((piece[0] for piece in weights))
            second_w = tuple((piece[1] for piece in weights))
            sent = low(low_back(one_layer(first_w, hidden, segment) + probe))
            return (sent, one_layer(second_w, sent, segment))
        return lax.map(jax.checkpoint(per_sequence), (hidden_all, probe_all, flat_seg))
    (sent_all, final_all), pullback = jax.vjp(whole, params, flat_in, probes)
    grads, grad_in, grad_sent = pullback((jnp.zeros_like(sent_all), cotangent.astype(jnp.float32).reshape(flat_in.shape)))
    shape = (mb_count, seq_count, length, width)
    section_outputs = jnp.stack([sent_all.reshape(shape), final_all.reshape(shape)]).astype(jnp.bfloat16)
    input_grads = jnp.stack([grad_in.reshape(shape), grad_sent.reshape(shape)]).astype(jnp.bfloat16)
    return (section_outputs, input_grads, grads[0], grads[1], grads[2], grads[3], grads[4], grads[5], grads[6], grads[7], grads[8], grads[9], grads[10])
```

```python
import functools
import math

import jax
import jax.numpy as jnp
from jax import lax
from jax.experimental import pallas as pl
from jax.experimental.pallas import tpu as pltpu
from jax.sharding import PartitionSpec as P

HD = 64
QUERY_BLOCK = 128

norm_eps = 1e-05
LOW = jnp.bfloat16
WIDE = jnp.float32


def layer_norm(values, gain, bias):
    centre = jnp.mean(values, -1, keepdims=True)
    centered = values - centre
    spread = jnp.mean(centered * centered, -1, keepdims=True)
    return centered * lax.rsqrt(spread + norm_eps) * gain + bias


def smooth_gate(values):
    return jax.nn.gelu(values, approximate=True)


def times(left, right):
    return jnp.dot(left, right, preferred_element_type=WIDE)


def contract_rows(left, right):
    return lax.dot_general(
        left, right, (((0,), (0,)), ((), ())), preferred_element_type=WIDE
    )


def times_transpose(left, right):
    return lax.dot_general(
        left, right, (((1,), (1,)), ((), ())), preferred_element_type=WIDE
    )


def fill_order(place, span, pieces, scratch, offset, count, factor=None):
    for k, piece in enumerate(pieces):
        rows = pl.ds(pl.multiple_of((place ^ k) * span, span), span)
        for h in range(count):
            part = piece[:, offset + h * HD : offset + (h + 1) * HD]
            if factor is not None:
                part = part * jnp.asarray(factor, part.dtype)
            scratch[h, rows, :] = part


def write_mask(mask_ref, seg_row_ref, seg_col_ref, start, block, reach):
    same = seg_col_ref[start : start + block, :] == seg_row_ref[:, :reach]
    row = lax.broadcasted_iota(jnp.int32, (block, reach), 0) + start
    col = lax.broadcasted_iota(jnp.int32, (block, reach), 1)
    mask_ref[:, :reach] = jnp.where(same & (col <= row), 0.0, -1e30)


def mix_forward_kernel(count, span, scale, place_ref, seg_row_ref, seg_col_ref, *refs):
    shards = len(refs) // 2 - 3
    pieces = refs[:shards]
    outs = refs[shards : 2 * shards]
    lse_ref, q_s, k_s, v_s, o_s, mask_ref = refs[2 * shards :]
    place = place_ref[0]
    wide = count * HD
    fill_order(place, span, pieces, q_s, 0, count, scale)
    fill_order(place, span, pieces, k_s, wide, count)
    fill_order(place, span, pieces, v_s, 2 * wide, count)
    length = q_s.shape[1]
    block = min(QUERY_BLOCK, length)
    lane = lax.broadcasted_iota(jnp.int32, (block, 128), 1)
    for start in range(0, length, block):
        reach = start + block
        write_mask(mask_ref, seg_row_ref, seg_col_ref, start, block, reach)
        lse_ref[start:reach, :] = jnp.zeros((block, 128), WIDE)

        @pl.loop(0, count)
        def _(h):
            q = q_s[h, start:reach, :]
            scores = times_transpose(q, k_s[h, :reach, :]) + mask_ref[:, :reach]
            peak = jnp.max(scores, -1, keepdims=True)
            raised = jnp.exp(scores - peak)
            total = jnp.sum(raised, -1, keepdims=True)
            mixed = times(raised.astype(LOW), v_s[h, :reach, :])
            o_s[h, start:reach, :] = (mixed * (1.0 / total)).astype(LOW)
            lse_ref[start:reach, :] = jnp.where(
                lane == h, peak + jnp.log(total), lse_ref[start:reach, :]
            )

    for k, out in enumerate(outs):
        rows = pl.ds(pl.multiple_of((place ^ k) * span, span), span)
        for h in range(count):
            out[:, h * HD : (h + 1) * HD] = o_s[h, rows, :]


def mix_backward_kernel(count, span, scale, place_ref, seg_row_ref, seg_col_ref, lse_ref, *refs):
    shards = (len(refs) - 8) // 3
    pieces = refs[:shards]
    grads = refs[shards : 2 * shards]
    outs = refs[2 * shards : 3 * shards]
    q_s, k_s, v_s, g_s, dq_s, dk_s, dv_s, mask_ref = refs[3 * shards :]
    place = place_ref[0]
    wide = count * HD
    fill_order(place, span, pieces, q_s, 0, count, scale)
    fill_order(place, span, pieces, k_s, wide, count)
    fill_order(place, span, pieces, v_s, 2 * wide, count)
    fill_order(place, span, grads, g_s, 0, count)
    dk_s[...] = jnp.zeros_like(dk_s)
    dv_s[...] = jnp.zeros_like(dv_s)
    length = q_s.shape[1]
    block = min(QUERY_BLOCK, length)
    lane = lax.broadcasted_iota(jnp.int32, (block, 128), 1)
    for start in range(0, length, block):
        reach = start + block
        write_mask(mask_ref, seg_row_ref, seg_col_ref, start, block, reach)

        @pl.loop(0, count)
        def _(h):
            q = q_s[h, start:reach, :]
            g = g_s[h, start:reach, :]
            keys = k_s[h, :reach, :]
            lse = jnp.sum(
                jnp.where(lane == h, lse_ref[start:reach, :], 0.0), -1, keepdims=True
            )
            scores = times_transpose(q, keys) + mask_ref[:, :reach]
            probs = jnp.exp(scores - lse)
            grad_probs = times_transpose(g, v_s[h, :reach, :])
            inner = jnp.sum(probs * grad_probs, -1, keepdims=True)
            grad_scores = (probs * (grad_probs - inner)).astype(LOW)
            dq_s[h, start:reach, :] = (times(grad_scores, keys) * scale).astype(LOW)
            dk_s[h, :reach, :] += contract_rows(grad_scores, q)
            dv_s[h, :reach, :] += contract_rows(probs.astype(LOW), g)

    for k, out in enumerate(outs):
        rows = pl.ds(pl.multiple_of((place ^ k) * span, span), span)
        for h in range(count):
            out[:, h * HD : (h + 1) * HD] = dq_s[h, rows, :]
            out[:, wide + h * HD : wide + (h + 1) * HD] = dk_s[h, rows, :].astype(LOW)
            out[:, 2 * wide + h * HD : 2 * wide + (h + 1) * HD] = dv_s[h, rows, :].astype(LOW)


def in_vmem(amount):
    return [pl.BlockSpec(memory_space=pltpu.VMEM)] * amount


def mix_forward(place, segment, pieces, count):
    shards = len(pieces)
    span = pieces[0].shape[0]
    length = segment.shape[0]
    scale = 1.0 / math.sqrt(HD)
    block = min(QUERY_BLOCK, length)
    outs = pl.pallas_call(
        functools.partial(mix_forward_kernel, count, span, scale),
        out_shape=[jax.ShapeDtypeStruct((span, count * HD), LOW)] * shards
        + [jax.ShapeDtypeStruct((length, 128), WIDE)],
        in_specs=[pl.BlockSpec(memory_space=pltpu.SMEM)] + in_vmem(2 + shards),
        out_specs=in_vmem(shards + 1),
        scratch_shapes=[pltpu.VMEM((count, length, HD), LOW)] * 4
        + [pltpu.VMEM((block, length), WIDE)],
        compiler_params=pltpu.CompilerParams(vmem_limit_bytes=40 << 20),
        cost_estimate=pl.CostEstimate(
            flops=count * length * length * HD * 8,
            bytes_accessed=8 * length * count * HD,
            transcendentals=count * length * length,
        ),
        name="mix_forward",
    )(place.reshape(1), segment.reshape(1, length), segment.reshape(length, 1), *pieces)
    return outs[:shards], outs[shards]


def mix_backward(place, segment, lse, pieces, grads, count):
    shards = len(pieces)
    span = pieces[0].shape[0]
    length = segment.shape[0]
    scale = 1.0 / math.sqrt(HD)
    block = min(QUERY_BLOCK, length)
    return pl.pallas_call(
        functools.partial(mix_backward_kernel, count, span, scale),
        out_shape=[jax.ShapeDtypeStruct((span, 3 * count * HD), LOW)] * shards,
        in_specs=[pl.BlockSpec(memory_space=pltpu.SMEM)] + in_vmem(3 + 2 * shards),
        out_specs=in_vmem(shards),
        scratch_shapes=[pltpu.VMEM((count, length, HD), LOW)] * 5
        + [pltpu.VMEM((count, length, HD), WIDE)] * 2
        + [pltpu.VMEM((block, length), WIDE)],
        compiler_params=pltpu.CompilerParams(vmem_limit_bytes=40 << 20),
        cost_estimate=pl.CostEstimate(
            flops=count * length * length * HD * 20,
            bytes_accessed=16 * length * count * HD,
            transcendentals=count * length * length,
        ),
        name="mix_backward",
    )(
        place.reshape(1),
        segment.reshape(1, length),
        segment.reshape(length, 1),
        lse,
        *pieces,
        *grads,
    )


def exchange(pieces):
    shards = len(pieces)
    return [pieces[0]] + [
        lax.ppermute(pieces[k], "shard", [(i, i ^ k) for i in range(shards)])
        for k in range(1, shards)
    ]


def swap(block):
    return lax.ppermute(block, "section", [(0, 1), (1, 0)])


def in_order(blocks, place, axis):
    size = blocks[0].shape[axis]
    shape = list(blocks[0].shape)
    shape[axis] = size * len(blocks)
    whole = jnp.zeros(shape, blocks[0].dtype)
    for k, block in enumerate(blocks):
        whole = lax.dynamic_update_slice_in_dim(whole, block, (place ^ k) * size, axis)
    return whole


def to_layer_owner(block, layer):
    moved = lax.ppermute(block, "section", [(1 - layer, layer)])
    return block.astype(WIDE) + moved.astype(WIDE)


def sum_replicas(block, layer):
    dtype = block.dtype
    replicas = lax.axis_size("replica")
    if replicas != 4:
        return lax.psum(block, "replica").astype(WIDE)
    base = layer * replicas
    axes = ("section", "replica")

    def move(value, route):
        return lax.ppermute(value, axes, [(base + a, base + b) for a, b in route])

    inward = move(block, [(0, 1), (3, 2)])
    half = (block.astype(WIDE) + inward.astype(WIDE)).astype(dtype)
    across = move(half, [(1, 2), (2, 1)])
    total = (half.astype(WIDE) + across.astype(WIDE)).astype(dtype)
    outward = move(total, [(1, 0), (2, 3)])
    place = lax.axis_index("replica")
    return jnp.where((place == 0) | (place == 3), outward, total).astype(WIDE)


def local(
    inputs,
    cotangent,
    segments,
    ln1_gain,
    ln1_bias,
    w_qkv,
    w_out,
    out_bias,
    ln2_gain,
    ln2_bias,
    w_up,
    up_bias,
    w_down,
    down_bias,
):
    first = lax.axis_index("section") == 0
    place = lax.axis_index("shard")
    shards = lax.axis_size("shard")
    span, width = inputs.shape[2:]
    length = segments.shape[2]
    heads = width // HD
    count = -(-heads // shards)
    mine_wide = count * HD
    own_rows = ln1_gain.shape[1]
    own_hidden = up_bias.shape[1]
    hidden_rows = own_hidden // own_rows
    partners = range(shards)

    def pick(pair):
        return jnp.where(first, pair[0], pair[1])

    def by_layer(mine):
        other = swap(mine)
        return (jnp.where(first, mine, other), jnp.where(first, other, mine))

    fresh = pick((inputs[0, 0], inputs[1, 0]))
    segment = pick((segments[0, 0], segments[1, 0]))
    grad_last = pick((cotangent[0, 0], cotangent[1, 0]))

    vectors = jnp.concatenate(
        [ln1_gain, ln1_bias, out_bias, ln2_gain, ln2_bias, down_bias]
        + [up_bias.reshape(hidden_rows, own_rows)],
        0,
    )
    vectors = lax.all_gather(vectors, ("section", "shard"))
    vectors = vectors.reshape(2, shards, 6 + hidden_rows, own_rows)
    small = vectors[:, :, :6].transpose(0, 2, 1, 3).reshape(2, 6, width).astype(WIDE)
    hidden_bias = (
        lax.dynamic_index_in_dim(vectors, place, 1, False)[:, 6:]
        .reshape(2, own_hidden)
        .astype(WIDE)
    )

    qkv_columns = jnp.pad(
        w_qkv[0].reshape(own_rows, 3, width), ((0, 0), (0, 0), (0, shards * mine_wide - width))
    )
    qkv_pieces = [
        lax.dynamic_slice_in_dim(qkv_columns, (place ^ k) * mine_wide, mine_wide, 2).reshape(
            own_rows, 3 * mine_wide
        )
        for k in partners
    ]
    proj_qkv = by_layer(in_order(exchange(qkv_pieces), place, 0))
    chunks_first = exchange([fresh] * shards)
    proj_out = by_layer(in_order(exchange([w_out[0]] * shards), place, 0))
    up_pieces = [
        lax.dynamic_slice_in_dim(w_up[0], (place ^ k) * own_hidden, own_hidden, 1)
        for k in partners
    ]
    proj_up = by_layer(in_order(exchange(up_pieces), place, 0))
    proj_down = by_layer(w_down[0])

    def forward(layer, low_hidden, chunks):
        gain_one, bias_one, bias_out, gain_two, bias_two, bias_down = small[layer]
        normed = [
            layer_norm(chunk.astype(WIDE), gain_one, bias_one).astype(LOW) for chunk in chunks
        ]
        project = [times(chunk, proj_qkv[layer]).astype(LOW) for chunk in normed]
        mixed_parts, lse = mix_forward(place, segment, project, count)
        mixed = in_order(exchange(mixed_parts), place, 1)[:, :width]
        hidden = low_hidden.astype(WIDE)
        middle = hidden + times(mixed, proj_out[layer]) + bias_out
        normed_two = exchange(
            [layer_norm(middle, gain_two, bias_two).astype(LOW)] * shards
        )
        gate_in = [times(chunk, proj_up[layer]) + hidden_bias[layer] for chunk in normed_two]
        activated = [smooth_gate(chunk).astype(LOW) for chunk in gate_in]
        terms = [times(chunk, proj_down[layer]) for chunk in activated]
        terms = exchange([terms[0]] + [term.astype(LOW) for term in terms[1:]])
        result = middle + bias_down + sum(term.astype(WIDE) for term in terms)
        saved = (hidden, normed, project, lse, mixed, middle, normed_two, gate_in, activated)
        return result.astype(LOW), saved

    def backward(layer, grad_low, branch, saved):
        hidden, normed, project, lse, mixed, middle, normed_two, gate_in, activated = saved
        gain_one, bias_one, bias_out, gain_two, bias_two, bias_down = small[layer]
        grad_out = grad_low.astype(WIDE)
        grad_gate = [
            jax.vjp(smooth_gate, gate)[1](times_transpose(chunk, proj_down[layer]))[0].astype(LOW)
            for chunk, gate in zip(branch, gate_in)
        ]
        terms = [times_transpose(chunk, proj_up[layer]) for chunk in grad_gate]
        terms = exchange([terms[0]] + [term.astype(LOW) for term in terms[1:]])
        grad_normed_two = sum(term.astype(WIDE) for term in terms)
        norm_pull_two = jax.vjp(layer_norm, middle, gain_two, bias_two)[1]
        grad_mid, grad_gain_two, grad_bias_two = norm_pull_two(grad_normed_two)
        grad_middle = grad_out + grad_mid
        grad_attn = grad_middle.astype(LOW)
        grad_mixed = jnp.pad(
            times_transpose(grad_attn, proj_out[layer]).astype(LOW),
            ((0, 0), (0, shards * mine_wide - width)),
        )
        grad_mixed = exchange(
            [
                lax.dynamic_slice_in_dim(grad_mixed, (place ^ k) * mine_wide, mine_wide, 1)
                for k in partners
            ]
        )
        grad_project = mix_backward(place, segment, lse, project, grad_mixed, count)
        terms = [times_transpose(chunk, proj_qkv[layer]) for chunk in grad_project]
        terms = exchange([terms[0]] + [term.astype(LOW) for term in terms[1:]])
        grad_normed = sum(term.astype(WIDE) for term in terms)
        norm_pull_one = jax.vjp(layer_norm, hidden, gain_one, bias_one)[1]
        grad_hidden, grad_gain_one, grad_bias_one = norm_pull_one(grad_normed)
        grad_input = (grad_middle + grad_hidden).astype(LOW)

        def rows_product(left, right):
            return contract_rows(jnp.concatenate(left, 0), jnp.concatenate(right, 0)).astype(LOW)

        down_sum = to_layer_owner(rows_product(activated, branch), layer).astype(LOW)
        down_sum = sum_replicas(down_sum, layer)

        def rows_to_owner(value):
            value = to_layer_owner(value, layer).astype(LOW)
            return exchange(
                [
                    lax.dynamic_slice_in_dim(value, (place ^ k) * own_rows, own_rows, 0)
                    for k in partners
                ]
            )

        up_sum = [
            sum_replicas(piece, layer)
            for piece in rows_to_owner(rows_product(normed_two, grad_gate))
        ]
        out_terms = rows_to_owner(contract_rows(mixed, grad_attn).astype(LOW))
        out_sum = sum_replicas(sum(term.astype(WIDE) for term in out_terms).astype(LOW), layer)
        qkv_sum = [
            sum_replicas(piece, layer)
            for piece in rows_to_owner(rows_product(normed, grad_project))
        ]
        vector_terms = jnp.stack(
            [
                grad_gain_one,
                grad_bias_one,
                jnp.sum(grad_attn.astype(WIDE), 0),
                grad_gain_two,
                grad_bias_two,
                jnp.sum(grad_low.astype(WIDE), 0),
            ]
        )
        vector_terms = sum(
            exchange(
                [
                    lax.dynamic_slice_in_dim(vector_terms, (place ^ k) * own_rows, own_rows, 1)
                    for k in partners
                ]
            )
        )
        up_terms = sum(jnp.sum(chunk.astype(WIDE), 0) for chunk in grad_gate)
        vector_terms = jnp.concatenate(
            [vector_terms, up_terms.reshape(hidden_rows, own_rows)], 0
        )
        vector_sum = sum_replicas(to_layer_owner(vector_terms, layer), layer)
        return grad_input, (down_sum, up_sum, out_sum, qkv_sum, vector_sum)

    branch_last = exchange([grad_last] * shards)
    sent, saved_first = forward(0, fresh, chunks_first)
    chunks_second = exchange([sent] * shards)
    final, saved_second = forward(1, sent, chunks_second)
    grad_sent, sums_second = backward(1, grad_last, branch_last, saved_second)
    branch_first = exchange([grad_sent] * shards)
    grad_first, sums_first = backward(0, grad_sent, branch_first, saved_first)

    def both_micro(of_first, of_second):
        own = jnp.where(first, of_first, of_second)
        moved = swap(jnp.where(first, of_second, of_first))
        return jnp.where(first, jnp.stack([own, moved]), jnp.stack([moved, own]))[None, :, None]

    section_outputs = both_micro(sent, final)
    input_grads = both_micro(grad_first, grad_sent)

    down_sum, up_sum, out_sum, qkv_sum, vector_sum = jax.tree.map(
        lambda a, b: jnp.where(first, a, b), sums_first, sums_second
    )
    up_sum = in_order(up_sum, place, 1)
    qkv_sum = in_order(
        [piece.reshape(own_rows, 3, mine_wide) for piece in qkv_sum], place, 2
    )[:, :, :width].reshape(own_rows, 3 * width)
    return (
        section_outputs,
        input_grads,
        vector_sum[0:1],
        vector_sum[1:2],
        qkv_sum[None],
        out_sum[None],
        vector_sum[2:3],
        vector_sum[3:4],
        vector_sum[4:5],
        up_sum[None],
        vector_sum[6:].reshape(1, own_hidden),
        down_sum[None],
        vector_sum[5:6],
    )


def solution(mesh):
    return jax.shard_map(
        local,
        mesh=mesh,
        in_specs=(
            P(None, "replica", "shard", None),
            P(None, "replica", "shard", None),
            P(None, "replica", None),
            P("section", "shard"),
            P("section", "shard"),
            P("section", "shard", None),
            P("section", "shard", None),
            P("section", "shard"),
            P("section", "shard"),
            P("section", "shard"),
            P("section", "shard", None),
            P("section", "shard"),
            P("section", "shard", None),
            P("section", "shard"),
        ),
        out_specs=(
            P("section", None, "replica", "shard", None),
            P("section", None, "replica", "shard", None),
            P("section", "shard"),
            P("section", "shard"),
            P("section", "shard", None),
            P("section", "shard", None),
            P("section", "shard"),
            P("section", "shard"),
            P("section", "shard"),
            P("section", "shard", None),
            P("section", "shard"),
            P("section", "shard", None),
            P("section", "shard"),
        ),
        check_vma=False,
    )
```
